32 devices in a mesh: grp: 2 (over y), seq: 8 (over z, core), dp: 2 (over x).
Axes of the slice: x: 2, y: 2, z: 4, core: 2. Of those that a mesh axis runs over, the one named last changes fastest.
Arguments:
- queries: bfloat16 [8, 2048, 2048], P(('grp', 'dp'), 'seq'), may hold values from -26 to 26
- key_states: bfloat16 [8, 2048, 2048], P(('grp', 'dp'), 'seq'), may hold values from -26 to 26
- value_states: bfloat16 [8, 2048, 2048], P(('grp', 'dp'), 'seq'), may hold values from -6 to 6
- projector: bfloat16 [2048, 1536], P('seq'), may hold values from -0.125 to 0.125
- teacher: bfloat16 [8, 2048, 1536], P(('grp', 'dp'), 'seq'), may hold values from -6 to 6
- enc_gain: float32 [1536], replicated, may hold values from 0.1 to 1.9
- enc_bias: float32 [1536], replicated, may hold values from -3 to 3
- valid_len: int32 [8], replicated, may hold values from 1 to 2048, 12288 in all
Outputs:
- grad_queries: bfloat16 [8, 2048, 2048], P(('grp', 'dp'), 'seq')
- grad_keys: bfloat16 [8, 2048, 2048], P(('grp', 'dp'), 'seq')
- grad_values: bfloat16 [8, 2048, 2048], P(('grp', 'dp'), 'seq')
The draws below stay inside these ranges and needn't reach their ends.
Inputs may be any that keep to these rules, and one draw needn't show every extreme that they name: valid_len[b] counts the leading real tokens of image b; some image has all 2048.
All inputs are finite; a program needn't handle non-finite values.
Results may differ from the reference program's by a relative error of at most 0.025.
Values may be sent and summed in bfloat16 or wider, within the bound.
No kernel may reach another device: no remote copies, remote signals or barrier semaphores. Data moves between devices by JAX's collectives and lax.ppermute only.
A program may use at most 192 MiB of HBM per device.

```python
import math
import jax
import jax.numpy as jnp
import numpy as np
from jax import lax

HEADS = 16
HD = 128
ENC = 1536
S = 2048
DW = 2048
IMGS = 8


def draw_queries(key, part):
    key = jax.random.fold_in(key, 11)
    base = jax.random.normal(key, (IMGS, S, HEADS * HD), jnp.float32)
    return base.astype(jnp.bfloat16)


def draw_key_states(key, part):
    key = jax.random.fold_in(key, 23)
    base = jax.random.normal(key, (IMGS, S, HEADS * HD), jnp.float32)
    return base.astype(jnp.bfloat16)


def steps_of(key, shape, split, low, top_value):
    def one(axis_at, shards_of):
        draws = jax.random.uniform(jax.random.fold_in(jax.random.fold_in(key, 6), axis_at), (shards_of,), jnp.float32, low / len(split), top_value / len(split))
        return jnp.repeat(jnp.exp(draws), shape[axis_at] // shards_of).reshape((-1,) + (1,) * (len(shape) - axis_at - 1))

    loudness = one(*split[0])
    for cut in split[1:]:
        loudness = loudness * one(*cut)
    return loudness


def profile(amount, total, reach, skew):
    portions = [(1 << 20) // math.isqrt(standing ** skew) + 1 for standing in range(2, amount + 1)]
    spare, counts = total - reach - (amount - 1), [1] * (amount - 1)
    while spare > 0:
        free = [i for i in range(amount - 1) if counts[i] < reach]
        mass, left = sum([portions[i] for i in free]), spare
        for i in free:
            more = min(reach - counts[i], max(1, left * portions[i] // mass), spare)
            counts[i] = counts[i] + more
            spare = spare - more
    return np.array([reach] + counts)


def ragged_sizes(key, count, total, limit, lean):
    if count == 2:
        one = jax.random.randint(key, (), max(1, total - limit), min(limit, total - 1) + 1)
        return jnp.stack([one, total - one])
    lengths = jnp.asarray(profile(count, total, limit, lean), jnp.int32)
    pairs = (count - 1) // 2
    source_of, taker = lengths[1:1 + 2 * pairs:2], lengths[2:2 + 2 * pairs:2]
    slack = jnp.minimum(source_of - 1, limit - taker)
    passed = jax.random.randint(jax.random.fold_in(key, 1), (pairs,), 0, 1 << 20) % (slack + 1)
    lengths = lengths.at[1:1 + 2 * pairs:2].set(source_of - passed).at[2:2 + 2 * pairs:2].set(taker + passed)
    return lengths[jax.random.permutation(jax.random.fold_in(key, 2), count)]


def bell_draw(own_key, extent, deviation, reach, cuts=(), held_as=jnp.bfloat16):
    drawn = deviation * jax.random.normal(own_key, extent, jnp.float32)
    if cuts:
        drawn = drawn * steps_of(own_key, extent, cuts, -0.22, 0.18)
    return jnp.clip(drawn, -reach, reach).astype(held_as)


def setup_inputs(seed: int = 0) -> dict:
    seeds = jax.random.split(jax.random.key(seed), 9)
    queries = draw_queries(jax.random.fold_in(seeds[8], 71), 0)
    key_states = draw_key_states(jax.random.fold_in(seeds[8], 71), 0)
    value_states = bell_draw(seeds[2], (IMGS, S, DW), 1.0, 6.0, ((0, 4), (1, 8)))
    projector = bell_draw(seeds[3], (DW, ENC), DW ** -0.5, 0.125, ((0, 8),))
    teacher = bell_draw(seeds[4], (IMGS, S, ENC), 1.0, 6.0, ((0, 4), (1, 8)))
    enc_gain = jnp.clip(1.0 + 0.18 * jax.random.normal(seeds[5], (ENC,), jnp.float32), 0.1, 1.9)
    enc_bias = bell_draw(seeds[6], (ENC,), 0.5, 3.0, (), jnp.float32)
    valid_len = ragged_sizes(seeds[7], IMGS, IMGS * S * 3 // 4, S, 1).astype(jnp.int32)
    return {"queries": queries, "key_states": key_states, "value_states": value_states, "projector": projector, "teacher": teacher, "enc_gain": enc_gain, "enc_bias": enc_bias, "valid_len": valid_len}


EPS = 1e-06
COEF = 2048.0

def layer_norm(rows, gain, bias):
    data = rows.astype(jnp.float32)
    center = data - lax.optimization_barrier(jnp.mean(data, axis=-1, keepdims=True))
    spread = lax.optimization_barrier(jnp.mean(center * center, axis=-1, keepdims=True))
    return center * lax.rsqrt(spread + EPS) * gain.astype(jnp.float32) + bias.astype(jnp.float32)

def cosine_grad(aligned, target, keep):
    tgt = target.astype(jnp.float32)
    width = aligned.shape[-1]
    inner = lax.optimization_barrier(jnp.mean(aligned * tgt, axis=-1, keepdims=True))
    own = lax.optimization_barrier(jnp.mean(aligned * aligned, axis=-1, keepdims=True)) + EPS
    other = lax.optimization_barrier(jnp.mean(tgt * tgt, axis=-1, keepdims=True)) + EPS
    inverse = lax.rsqrt(own * other)
    cosine = inner * inverse
    return -COEF / width * keep[..., None] * (tgt * inverse - cosine / own * aligned)

def reference(queries, key_states, value_states, projector, teacher, enc_gain, enc_bias, valid_len):
    target = layer_norm(jnp.roll(teacher, IMGS // 2, axis=0), enc_gain, enc_bias).astype(jnp.bfloat16)
    scale = HD ** (-0.5)
    positions = jnp.arange(S, dtype=jnp.int32)

    def split_heads(rows):
        return rows.reshape(S, HEADS, HD).transpose(1, 0, 2).astype(jnp.float32)

    def join_heads(block):
        return block.transpose(1, 0, 2).reshape(S, HEADS * HD)

    def per_image(items):
        query, keyrow, value, tgt, length = items
        keep = positions < length
        qh = split_heads(query)
        kh = split_heads(keyrow)
        vh = split_heads(value)
        scores = jnp.einsum('hid,hjd->hij', qh, kh) * scale
        scores = jnp.where(keep[None, None, :], scores, -jnp.inf)
        top = lax.optimization_barrier(jnp.max(scores, axis=-1, keepdims=True))
        expo = jnp.exp(scores - top)
        probs = expo / lax.optimization_barrier(jnp.sum(expo, axis=-1, keepdims=True))
        probs_b = probs.astype(jnp.bfloat16).astype(jnp.float32)
        attended = jnp.einsum('hij,hjd->hid', probs_b, vh).astype(jnp.bfloat16)
        aligned = jnp.dot(join_heads(attended), projector, preferred_element_type=jnp.float32)
        grad_aligned = cosine_grad(aligned, tgt, keep.astype(jnp.float32)).astype(jnp.bfloat16)
        grad_att = jnp.dot(grad_aligned, projector.T, preferred_element_type=jnp.float32).astype(jnp.bfloat16)
        gh = split_heads(grad_att)
        grad_v = jnp.einsum('hij,hid->hjd', probs_b, gh).astype(jnp.bfloat16)
        grad_probs = jnp.einsum('hid,hjd->hij', gh, vh)
        delta = lax.optimization_barrier(jnp.sum(probs * grad_probs, axis=-1, keepdims=True))
        grad_scores = (probs * (grad_probs - delta) * scale).astype(jnp.bfloat16).astype(jnp.float32)
        grad_q = jnp.einsum('hij,hjd->hid', grad_scores, kh).astype(jnp.bfloat16)
        grad_k = jnp.einsum('hij,hid->hjd', grad_scores, qh).astype(jnp.bfloat16)
        return (join_heads(grad_q), join_heads(grad_k), join_heads(grad_v))
    grad_queries, grad_keys, grad_values = lax.map(per_image, (queries, key_states, value_states, target, valid_len))
    return (grad_queries, grad_keys, grad_values)
```

```python
import functools

import jax
import jax.numpy as jnp
from jax import lax
from jax.experimental import pallas as pl
from jax.experimental.pallas import tpu as pltpu
from jax.sharding import PartitionSpec as P

HD = 128
EPS = 1e-06
COEF = 2048.0
SCALE = HD ** (-0.5)
LOG2E = 1.4426950408889634
NEG = -1e30
NT = (((1,), (1,)), ((), ()))
NN = (((1,), (0,)), ((), ()))
VMEM_LIMIT = 62 * 1024 * 1024
VMEM_LIMIT_PLACE = 16 * 1024 * 1024
WEIGHT = 16


def dot(a, b, dims):
    return lax.dot_general(a, b, dims, preferred_element_type=jnp.float32)


def cost(flops, data, exps=0):
    return pl.CostEstimate(
        flops=WEIGHT * flops, bytes_accessed=WEIGHT * data, transcendentals=WEIGHT * exps
    )


def from_partner(value, axis, apart):
    return lax.ppermute(value, axis, [(i, i ^ 1 << apart) for i in range(lax.axis_size(axis))])


def exchange(slabs):
    if len(slabs) == 1:
        return [lax.all_to_all(slabs[0], "seq", split_axis=0, concat_axis=0, tiled=True)]
    ranks = len(slabs)
    return [
        lax.ppermute(slab, "seq", [(i, i ^ s) for i in range(ranks)]) if s else slab
        for s, slab in enumerate(slabs)
    ]


def slab_shapes(split, ranks, shape, dtype=jnp.bfloat16):
    if split:
        return [jax.ShapeDtypeStruct(shape, dtype)] * ranks
    return [jax.ShapeDtypeStruct((ranks,) + shape, dtype)]


def slab_specs(split, ranks, shape, index):
    if split:
        return [pl.BlockSpec(shape, index)] * ranks
    return [pl.BlockSpec((ranks,) + shape, lambda *at: (0,) + index(*at))]


def each_slab(refs, ranks, me):
    if len(refs) == 1:
        return [(s, refs[0].at[s]) for s in range(ranks)]
    return [(s ^ me, refs[s]) for s in range(ranks)]


def unread(deps):
    return [pl.BlockSpec(memory_space=pl.ANY)] * len(deps)


def image_at(plan, len_ref, me_ref):
    c, chunks, images = plan
    if chunks != 2 or images != 1:
        return c * images
    swap = (len_ref[me_ref[2] + 1] < len_ref[me_ref[2]]).astype(jnp.int32)
    return 1 - swap if c else swap


def span(rank, size):
    if isinstance(rank, int):
        return pl.ds(rank * size, size)
    return pl.ds(pl.multiple_of(rank * size, size), size)


def pack_kernel(per, parts, _, __, *refs):
    ins, out = refs[:parts], refs[-1]
    for part in range(parts):
        for r in range(out.shape[0]):
            for j in range(per):
                at = (r * per + j) * HD
                out[r, part, j] = ins[part][0, :, at : at + HD]


def pack_slabs_kernel(per, parts, ranks, _, __, *refs):
    ins, outs = refs[: ranks * parts], refs[-ranks:]
    for s in range(ranks):
        for part in range(parts):
            for j in range(per):
                outs[s][part, j] = ins[s * parts + part][0, :, j * HD : (j + 1) * HD]


def pack(arrays, plan, ranks, per, split, where, deps):
    seg, width = arrays[0].shape[1:]
    parts, images = len(arrays), plan[2]
    ranks_image = ranks // images
    if split:
        steps = 2 if seg % 32 == 0 else 1
        rows = seg // steps

        def column(s):
            return pl.BlockSpec(
                (1, rows, per * HD),
                lambda h, n, m: (
                    image_at(plan, n, m) + lax.div(m[0] ^ s, ranks_image),
                    h,
                    lax.rem(m[0] ^ s, ranks_image),
                ),
            )

        kernel = functools.partial(pack_slabs_kernel, per, parts, ranks)
        operands = list(arrays) * ranks
        in_specs = [column(s) for s in range(ranks) for _ in range(parts)]
        out_specs = slab_specs(split, ranks, (parts, per, rows, HD), lambda h, n, m: (0, 0, h, 0))
    else:
        group = 2 if ranks_image % 2 == 0 else 1
        steps_image = ranks_image // group
        steps = ranks // group
        kernel = functools.partial(pack_kernel, per, parts)
        operands = list(arrays)
        in_specs = [
            pl.BlockSpec(
                (1, seg, group * per * HD),
                lambda s, n, m: (
                    image_at(plan, n, m) + lax.div(s, steps_image),
                    0,
                    lax.rem(s, steps_image),
                ),
            )
        ] * parts
        out_specs = [
            pl.BlockSpec((group, parts, per, seg, HD), lambda s, n, m: (s, 0, 0, 0, 0))
        ]
    return pl.pallas_call(
        kernel,
        grid_spec=pltpu.PrefetchScalarGridSpec(
            num_scalar_prefetch=2,
            grid=(steps,),
            in_specs=in_specs + unread(deps),
            out_specs=out_specs,
        ),
        out_shape=slab_shapes(split, ranks, (parts, per, seg, HD)),
        cost_estimate=cost(0, 4 * parts * images * seg * width),
        compiler_params=pltpu.CompilerParams(vmem_limit_bytes=VMEM_LIMIT),
        name="pack",
    )(*where, *operands, *deps)


def unpack_kernel(per, parts, _, __, *refs):
    src, outs = refs[0], refs[-parts:]
    for part in range(parts):
        for r in range(src.shape[0]):
            for j in range(per):
                at = (r * per + j) * HD
                outs[part][0, :, at : at + HD] = src[r, part, j]


def unpack(block, plan, count, where, held, deps):
    ranks, parts, per, seg, _ = block.shape
    images = plan[2]
    width = ranks * per // images * HD
    ranks_image = ranks // images
    group = 2 if ranks_image % 2 == 0 else 1
    steps_image = ranks_image // group
    held = list(held)

    def at(s, n, m):
        image = image_at(plan, n, m) + lax.div(s, steps_image)
        return image, 0, lax.rem(s, steps_image)

    return pl.pallas_call(
        functools.partial(unpack_kernel, per, parts),
        grid_spec=pltpu.PrefetchScalarGridSpec(
            num_scalar_prefetch=2,
            grid=(ranks // group,),
            in_specs=[
                pl.BlockSpec((group, parts, per, seg, HD), lambda s, n, m: (s, 0, 0, 0, 0))
            ]
            + unread(held)
            + unread(deps),
            out_specs=[pl.BlockSpec((1, seg, group * per * HD), at)] * parts,
        ),
        out_shape=[jax.ShapeDtypeStruct((count, seg, width), jnp.bfloat16)] * parts,
        input_output_aliases={3 + i: i for i in range(len(held))},
        cost_estimate=cost(0, 4 * parts * images * seg * width),
        compiler_params=pltpu.CompilerParams(vmem_limit_bytes=VMEM_LIMIT),
        name="unpack",
    )(*where, block, *held, *deps)


def place_kernel(per, parts, _, __, src, *refs):
    for part in range(parts):
        for j in range(per):
            refs[parts + part][0, :, j * HD : (j + 1) * HD] = src[part, j]


def place(slab, distance, plan, count, ranks, where, held):
    parts, per, seg, _ = slab.shape
    images = plan[2]
    width = ranks * per // images * HD
    ranks_image = ranks // images

    def at(s, n, m):
        owner = m[0] ^ distance
        image = image_at(plan, n, m) + lax.div(owner, ranks_image)
        return image, 0, lax.rem(owner, ranks_image)

    return pl.pallas_call(
        functools.partial(place_kernel, per, parts),
        grid_spec=pltpu.PrefetchScalarGridSpec(
            num_scalar_prefetch=2,
            grid=(1,),
            in_specs=[pl.BlockSpec((parts, per, seg, HD), lambda s, n, m: (0, 0, 0, 0))]
            + unread(held),
            out_specs=[pl.BlockSpec((1, seg, per * HD), at)] * parts,
        ),
        out_shape=[jax.ShapeDtypeStruct((count, seg, width), jnp.bfloat16)] * parts,
        input_output_aliases={3 + i: i for i in range(parts)},
        cost_estimate=cost(0, 4 * parts * per * seg * HD),
        compiler_params=pltpu.CompilerParams(vmem_limit_bytes=VMEM_LIMIT_PLACE),
        name="place",
    )(*where, slab, *held)


def tiles_of(total, seg):
    return min(total, max(512, seg)), min(total, max(512, seg))


def for_each_count(count, most, body):
    for n in range(1, most + 1):
        pl.when(count == n)(functools.partial(body, n))


def pair_length(len_ref, me_ref, plan, heads):
    pair = me_ref[0] * pl.num_programs(0) + pl.program_id(0)
    return len_ref[me_ref[2] + image_at(plan, len_ref, me_ref) + lax.div(pair, heads)]


def forward_kernel(sizes, len_ref, me_ref, *refs):
    n_slabs, n_deps, ranks, seg, tq, tk, plan, heads = sizes
    ins, refs = refs[:n_slabs], refs[n_slabs + n_deps :]
    outs = refs[:n_slabs]
    st_ref, ot_ref, q_ref, k_ref, v_ref, vt_ref, even_ref, odd_ref, o_ref = refs[n_slabs:]
    length = pair_length(len_ref, me_ref, plan, heads)
    total = ranks * seg
    for r, slab in each_slab(ins, ranks, me_ref[0]):
        rows = span(r, seg)
        q_ref[rows, :] = slab[0]
        k_ref[rows, :] = slab[1]
        v_ref[rows, :] = slab[2]
    for t in range(total // tk):
        vt_ref[:HD, t * tk : (t + 1) * tk] = v_ref[t * tk : (t + 1) * tk, :].T
    vt_ref[HD:, :] = jnp.ones_like(vt_ref[HD:, :])
    nq = lax.div(length + (tq - 1), tq)
    nk = lax.div(length + (tk - 1), tk)

    last_step = total // tq - 1

    def with_tiles(tiles):
        def scores(i, s_ref, t, top):
            rows = slice(t * tk, (t + 1) * tk)
            s = dot(k_ref[rows, :], q_ref[span(i, tq), :], NT)
            if t == tiles - 1:
                row = lax.broadcasted_iota(jnp.int32, (tk, tq), 0) + t * tk
                s = jnp.where(row < length, s, NEG)
            s_ref[rows, :] = s
            high = jnp.max(s, axis=0, keepdims=True)
            return high if top is None else jnp.maximum(top, high)

        def q_step(i, top, s_ref, next_ref):
            acc, next_top = jnp.zeros((vt_ref.shape[0], tq), jnp.float32), None
            for t in range(tiles):
                rows = slice(t * tk, (t + 1) * tk)
                next_top = scores(jnp.minimum(i + 1, last_step), next_ref, t, next_top)
                p = jnp.exp2((s_ref[rows, :] - top) * (SCALE * LOG2E))
                acc = acc + dot(vt_ref[:, rows], p.astype(jnp.bfloat16), NN)
            denom = acc[HD : HD + 1]
            out = acc[:HD] * (1.0 / denom)
            st_ref[0:1, span(i, tq)] = top * (SCALE * LOG2E) + jnp.log2(denom)
            ot_ref[:, span(i, tq)] = out
            o_ref[span(i, tq), :] = out.T.astype(jnp.bfloat16)
            return next_top

        def two_steps(pair, top):
            top = q_step(2 * pair, top, even_ref, odd_ref)
            if last_step == 0:
                return top
            return q_step(2 * pair + 1, top, odd_ref, even_ref)

        top = None
        for t in range(tiles):
            top = scores(0, even_ref, t, top)
        lax.fori_loop(0, lax.div(nq + 1, 2), two_steps, top)

    for_each_count(nk, total // tk, with_tiles)

    def blank(i, _):
        o_ref[span(i, tq), :] = jnp.zeros((tq, HD), jnp.bfloat16)
        return 0

    lax.fori_loop(nq, total // tq, blank, 0)
    for r, slab in each_slab(outs, ranks, me_ref[0]):
        slab[...] = o_ref[span(r, seg), :]


def forward(qkv, plan, ranks, where, deps):
    split = len(qkv) > 1
    per, seg = qkv[0].shape[-3:-1]
    heads = ranks * per // plan[2]
    total = ranks * seg
    tq, tk = tiles_of(total, seg)
    *attended, stats, kept = pl.pallas_call(
        functools.partial(forward_kernel, (len(qkv), len(deps), ranks, seg, tq, tk, plan, heads)),
        grid_spec=pltpu.PrefetchScalarGridSpec(
            num_scalar_prefetch=2,
            grid=(per,),
            in_specs=slab_specs(split, ranks, (3, None, seg, HD), lambda p, n, m: (0, p, 0, 0))
            + unread(deps),
            out_specs=slab_specs(split, ranks, (None, seg, HD), lambda p, n, m: (p, 0, 0))
            + [
                pl.BlockSpec((None, 8, total), lambda p, n, m: (p, 0, 0)),
                pl.BlockSpec((None, HD, total), lambda p, n, m: (p, 0, 0)),
            ],
            scratch_shapes=[pltpu.VMEM((total, HD), jnp.bfloat16)] * 3
            + [
                pltpu.VMEM((HD + 16, total), jnp.bfloat16),
                pltpu.VMEM((total, tq), jnp.float32),
                pltpu.VMEM((total, tq), jnp.float32),
                pltpu.VMEM((total, HD), jnp.bfloat16),
            ],
        ),
        out_shape=slab_shapes(split, ranks, (per, seg, HD))
        + [
            jax.ShapeDtypeStruct((per, 8, total), jnp.float32),
            jax.ShapeDtypeStruct((per, HD, total), jnp.float32),
        ],
        cost_estimate=cost(8 * per * total * total * HD, 8 * per * total * HD, per * total * total),
        compiler_params=pltpu.CompilerParams(vmem_limit_bytes=VMEM_LIMIT),
        name="attend_fwd",
    )(*where, *qkv, *deps)
    return attended, (stats, kept)


def backward_kernel(sizes, len_ref, me_ref, *refs):
    n_slabs, n_deps, ranks, seg, tq, tk, plan, heads = sizes
    ins, g_ins = refs[:n_slabs], refs[n_slabs : 2 * n_slabs]
    st_ref, ot_ref = refs[2 * n_slabs : 2 * n_slabs + 2]
    refs = refs[2 * n_slabs + 2 + n_deps :]
    outs = refs[:n_slabs]
    q_ref, k_ref, v_ref, g_ref, kt_ref, dq_ref, dk_ref, dv_ref = refs[n_slabs:]
    length = pair_length(len_ref, me_ref, plan, heads)
    total = ranks * seg
    for r, slab in each_slab(ins, ranks, me_ref[0]):
        rows = span(r, seg)
        q_ref[rows, :] = slab[0]
        k_ref[rows, :] = slab[1]
        v_ref[rows, :] = slab[2]
    for r, slab in each_slab(g_ins, ranks, me_ref[0]):
        g_ref[span(r, seg), :] = slab[...]
    for t in range(total // tk):
        kt_ref[:, t * tk : (t + 1) * tk] = k_ref[t * tk : (t + 1) * tk, :].T
    nq = lax.div(length + (tq - 1), tq)
    nk = lax.div(length + (tk - 1), tk)
    dk_ref[...] = jnp.zeros_like(dk_ref)
    dv_ref[...] = jnp.zeros_like(dv_ref)

    def with_tiles(tiles):
        def q_step(i, _):
            q = q_ref[span(i, tq), :]
            g = g_ref[span(i, tq), :]
            offset = st_ref[0:1, span(i, tq)]
            delta = jnp.sum(
                ot_ref[:, span(i, tq)] * g.astype(jnp.float32).T, axis=0, keepdims=True
            )
            dq = jnp.zeros((HD, tq), jnp.float32)

            part = tk // 2
            parts = [slice(at, at + part) for at in range(0, tiles * tk, part)]

            def products(rows):
                return dot(k_ref[rows, :], q, NT), dot(v_ref[rows, :], g, NT)

            ahead = products(parts[0])
            for t, rows in enumerate(parts):
                s, dp = ahead
                if t + 1 < len(parts):
                    ahead = products(parts[t + 1])
                s = s * (SCALE * LOG2E) - offset
                if t + 2 >= len(parts):
                    row = lax.broadcasted_iota(jnp.int32, (part, tq), 0) + rows.start
                    s = jnp.where(row < length, s, NEG)
                p = jnp.exp2(s)
                ds = (p * (dp - delta)).astype(jnp.bfloat16)
                dv_ref[rows, :] += dot(p.astype(jnp.bfloat16), g, NN)
                dk_ref[rows, :] += dot(ds, q, NN)
                dq = dq + dot(kt_ref[:, rows], ds, NN)
            dq_ref[span(i, tq), :] = (dq.T * SCALE).astype(jnp.bfloat16)
            return 0

        lax.fori_loop(0, nq, q_step, 0)

    for_each_count(nk, total // tk, with_tiles)

    def blank(i, _):
        dq_ref[span(i, tq), :] = jnp.zeros((tq, HD), jnp.bfloat16)
        return 0

    lax.fori_loop(nq, total // tq, blank, 0)
    for r, slab in each_slab(outs, ranks, me_ref[0]):
        rows = span(r, seg)
        slab[0] = dq_ref[rows, :]
        slab[1] = (dk_ref[rows, :] * SCALE).astype(jnp.bfloat16)
        slab[2] = dv_ref[rows, :].astype(jnp.bfloat16)


def backward(qkv, g_in, kept, plan, ranks, where, deps):
    split = len(qkv) > 1
    per, seg = qkv[0].shape[-3:-1]
    heads = ranks * per // plan[2]
    total = ranks * seg
    tq, tk = tiles_of(total, seg)
    block = (3, None, seg, HD)
    return pl.pallas_call(
        functools.partial(backward_kernel, (len(qkv), len(deps), ranks, seg, tq, tk, plan, heads)),
        grid_spec=pltpu.PrefetchScalarGridSpec(
            num_scalar_prefetch=2,
            grid=(per,),
            in_specs=slab_specs(split, ranks, block, lambda p, n, m: (0, p, 0, 0))
            + slab_specs(split, ranks, (None, seg, HD), lambda p, n, m: (p, 0, 0))
            + [
                pl.BlockSpec((None, 8, total), lambda p, n, m: (p, 0, 0)),
                pl.BlockSpec((None, HD, total), lambda p, n, m: (p, 0, 0)),
            ]
            + unread(deps),
            out_specs=slab_specs(split, ranks, block, lambda p, n, m: (0, p, 0, 0)),
            scratch_shapes=[pltpu.VMEM((total, HD), jnp.bfloat16)] * 4
            + [
                pltpu.VMEM((HD, total), jnp.bfloat16),
                pltpu.VMEM((total, HD), jnp.bfloat16),
                pltpu.VMEM((total, HD), jnp.float32),
                pltpu.VMEM((total, HD), jnp.float32),
            ],
        ),
        out_shape=slab_shapes(split, ranks, (3, per, seg, HD)),
        cost_estimate=cost(20 * per * total * total * HD, 14 * per * total * HD, per * total * total),
        compiler_params=pltpu.CompilerParams(vmem_limit_bytes=VMEM_LIMIT),
        name="attend_bwd",
    )(*where, *qkv, *g_in, *kept, *deps)


def gather_rows(rows, deps):
    planes = lax.axis_size("grp") * lax.axis_size("dp")
    enc = rows.shape[1]
    shares = 1
    while shares * 2 <= planes and enc % (shares * 2 * HD) == 0:
        shares *= 2
    plane = lax.axis_index("grp") * lax.axis_size("dp") + lax.axis_index("dp")
    wide = enc // shares
    mine = lax.dynamic_slice_in_dim(rows, (plane % shares) * wide, wide, axis=1)
    along = after(lax.all_gather(mine, "seq", axis=0, tiled=True), deps)
    groups = [list(range(at, at + shares)) for at in range(0, planes, shares)]
    return lax.all_gather(
        along, ("grp", "dp"), axis=0, axis_index_groups=groups if len(groups) > 1 else None
    )


def norm_kernel(t_ref, gain_ref, bias_ref, _, out_ref):
    data = t_ref[...].astype(jnp.float32)
    center = data - jnp.mean(data, axis=-1, keepdims=True)
    spread = jnp.mean(center * center, axis=-1, keepdims=True)
    normed = center * lax.rsqrt(spread + EPS) * gain_ref[...] + bias_ref[...]
    out_ref[...] = normed.astype(jnp.bfloat16)


def layer_norm(rows, gain, bias, dep):
    count, seg, enc = rows.shape
    block = pl.BlockSpec((None, seg, enc), lambda b: (b, 0, 0))
    vector = pl.BlockSpec((1, enc), lambda b: (0, 0))
    return pl.pallas_call(
        norm_kernel,
        grid=(count,),
        in_specs=[block, vector, vector] + unread([dep]),
        out_specs=block,
        out_shape=jax.ShapeDtypeStruct(rows.shape, jnp.bfloat16),
        cost_estimate=cost(10 * rows.size, 4 * rows.size),
        compiler_params=pltpu.CompilerParams(vmem_limit_bytes=VMEM_LIMIT),
        name="layer_norm",
    )(rows, gain.reshape(1, -1), bias.reshape(1, -1), dep)


def after_kernel(*_):
    pass


def after(value, deps):
    return pl.pallas_call(
        after_kernel,
        in_specs=unread([value, *deps]),
        out_specs=pl.BlockSpec(memory_space=pl.ANY),
        out_shape=jax.ShapeDtypeStruct(value.shape, value.dtype),
        input_output_aliases={0: 0},
        cost_estimate=cost(0, 0),
        name="after",
    )(value, *deps)


def head_kernel(sizes, len_ref, me_ref, *refs):
    n_slabs, ranks, plan, per, seg = sizes
    images = plan[2]
    image = image_at(plan, len_ref, me_ref)
    ins = refs[:n_slabs]
    w_ref, t_ref = refs[n_slabs : n_slabs + 2]
    outs, rows_ref = refs[-1 - n_slabs : -1], refs[-1]
    heads = ranks * per // images

    def place_of(r, j):
        pair = r * per + j
        return span(lax.div(pair, heads), seg), span(lax.rem(pair, heads), HD)

    for r, slab in each_slab(ins, ranks, me_ref[0]):
        for j in range(per):
            rows, cols = place_of(jnp.int32(r), j)
            rows_ref[rows, cols] = slab[j]
    shares, _, wide = w_ref.shape
    for b in range(images):
        rows = rows_ref[b * seg : (b + 1) * seg, :]
        aligned = jnp.concatenate([dot(rows, w_ref[part], NN) for part in range(shares)], axis=1)
        tgt = t_ref[b].astype(jnp.float32)
        width = aligned.shape[-1]
        inner = jnp.mean(aligned * tgt, axis=-1, keepdims=True)
        own = jnp.mean(aligned * aligned, axis=-1, keepdims=True) + EPS
        other = jnp.mean(tgt * tgt, axis=-1, keepdims=True) + EPS
        inverse = lax.rsqrt(own * other)
        cosine = inner * inverse
        row = lax.broadcasted_iota(jnp.int32, (seg, 1), 0) + me_ref[1]
        keep = jnp.where(row < len_ref[me_ref[2] + image + b], -COEF / width, 0.0)
        grad = (keep * (tgt * inverse - cosine / own * aligned)).astype(jnp.bfloat16)
        grad_rows = dot(grad[:, :wide], w_ref[0], NT)
        for part in range(1, shares):
            grad_rows += dot(grad[:, part * wide : (part + 1) * wide], w_ref[part], NT)
        rows_ref[b * seg : (b + 1) * seg, :] = grad_rows.astype(jnp.bfloat16)
    for r, slab in each_slab(outs, ranks, me_ref[0]):
        for j in range(per):
            rows, cols = place_of(jnp.int32(r), j)
            slab[j] = rows_ref[rows, cols]


def align_head(back, whole, target, plan, ranks, where, deps):
    split = len(back) > 1
    per, seg = back[0].shape[-3:-1]
    shares, width, wide = whole.shape
    enc, images = shares * wide, plan[2]
    slabs = slab_specs(split, ranks, (per, seg, HD), lambda b, n, m: (0, 0, 0))
    return pl.pallas_call(
        functools.partial(head_kernel, (len(back), ranks, plan, per, seg)),
        grid_spec=pltpu.PrefetchScalarGridSpec(
            num_scalar_prefetch=2,
            grid=(1,),
            in_specs=slabs
            + [
                pl.BlockSpec((shares, width, wide), lambda b, n, m: (0, 0, 0)),
                pl.BlockSpec((images, seg, enc), lambda b, n, m: (lax.div(image_at(plan, n, m), images), 0, 0)),
            ]
            + unread(deps),
            out_specs=slabs,
            scratch_shapes=[pltpu.VMEM((images * seg, width), jnp.bfloat16)],
        ),
        out_shape=slab_shapes(split, ranks, (per, seg, HD)),
        cost_estimate=cost(
            4 * images * seg * width * enc, 2 * width * enc + 10 * images * seg * width, 0
        ),
        compiler_params=pltpu.CompilerParams(vmem_limit_bytes=VMEM_LIMIT),
        name="align_head",
    )(*where, *back, whole, target, *deps)


def shards(queries, key_states, value_states, projector, teacher, enc_gain, enc_bias, valid_len):
    ranks = lax.axis_size("seq")
    count, seg, width = queries.shape
    heads = width // HD
    images = 1
    while images * heads % ranks:
        images *= 2
    chunks = count // images
    per = images * heads // ranks
    rank = lax.axis_index("seq").astype(jnp.int32)

    first_image = (lax.axis_index("grp") * lax.axis_size("dp") + lax.axis_index("dp")) * count
    where = (valid_len, jnp.stack([rank, rank * seg, first_image.astype(jnp.int32)]))
    plans = [(c, chunks, images) for c in range(chunks)]
    split = [chunks > 1 and c == chunks - 1 for c in range(chunks)]

    arrays = (queries, key_states, value_states)
    packed = []
    for c in range(chunks):
        deps = [slabs[0] for slabs in packed]
        packed.append(pack(arrays, plans[c], ranks, per, split[c], where, deps))
    normed = layer_norm(teacher, enc_gain, enc_bias, packed[0][0])
    target = from_partner(normed, "grp", 0)
    whole = gather_rows(projector, packed[-1][:1])

    def ahead(near, made, c, also=[]):
        if not split[-1]:
            return []
        return made[c - 1][:1] if split[c] else near[-1][:3] + also

    qkv = [exchange(slabs) for slabs in packed]
    attended, kept = [], []
    for c in range(chunks):
        slabs, state = forward(qkv[c], plans[c], ranks, where, ahead(qkv, attended, c, [target]))
        kept.append(state)
        attended.append(slabs)
    back = [exchange(slabs) for slabs in attended]
    grad_rows = []
    for c in range(chunks):
        deps = ahead(back, grad_rows, c)
        grad_rows.append(align_head(back[c], whole, target, plans[c], ranks, where, deps))
    g_in = [exchange(slabs) for slabs in grad_rows]
    grads = []
    for c in range(chunks):
        deps = ahead(g_in, grads, c)
        grads.append(backward(qkv[c], g_in[c], kept[c], plans[c], ranks, where, deps))
    grads = [exchange(slabs) for slabs in grads]
    outs = ()
    for c in range(chunks):
        if not split[c]:
            outs = unpack(grads[c][0], plans[c], count, where, outs, ahead(grads, None, c))
            continue
        for s, slab in enumerate(grads[c]):
            outs = place(slab, s, plans[c], count, ranks, where, outs)
    return tuple(outs)


def solution(mesh):
    return jax.shard_map(
        shards,
        mesh=mesh,
        in_specs=(
            P(("grp", "dp"), "seq", None),
            P(("grp", "dp"), "seq", None),
            P(("grp", "dp"), "seq", None),
            P("seq", None),
            P(("grp", "dp"), "seq", None),
            P(),
            P(),
            P(),
        ),
        out_specs=(
            P(("grp", "dp"), "seq", None),
            P(("grp", "dp"), "seq", None),
            P(("grp", "dp"), "seq", None),
        ),
        check_vma=False,
    )
```

```python
import functools

import jax
import jax.numpy as jnp
from jax import lax
from jax.experimental import pallas as pl
from jax.experimental.pallas import tpu as pltpu
from jax.sharding import PartitionSpec as P

HD = 128
EPS = 1e-06
COEF = 2048.0
SCALE = HD ** (-0.5)
LOG2E = 1.4426950408889634
NEG = -1e30
NT = (((1,), (1,)), ((), ()))
NN = (((1,), (0,)), ((), ()))
VMEM_LIMIT = 62 * 1024 * 1024
VMEM_LIMIT_PLACE = 16 * 1024 * 1024
WEIGHT = 16


def dot(a, b, dims):
    return lax.dot_general(a, b, dims, preferred_element_type=jnp.float32)


def cost(flops, data, exps=0):
    return pl.CostEstimate(
        flops=WEIGHT * flops, bytes_accessed=WEIGHT * data, transcendentals=WEIGHT * exps
    )


def from_partner(value, axis, apart):
    return lax.ppermute(value, axis, [(i, i ^ 1 << apart) for i in range(lax.axis_size(axis))])


def exchange(slabs):
    if len(slabs) == 1:
        return [lax.all_to_all(slabs[0], "seq", split_axis=0, concat_axis=0, tiled=True)]
    ranks = len(slabs)
    return [
        lax.ppermute(slab, "seq", [(i, i ^ s) for i in range(ranks)]) if s else slab
        for s, slab in enumerate(slabs)
    ]


def slab_shapes(split, ranks, shape, dtype=jnp.bfloat16):
    if split:
        return [jax.ShapeDtypeStruct(shape, dtype)] * ranks
    return [jax.ShapeDtypeStruct((ranks,) + shape, dtype)]


def slab_specs(split, ranks, shape, index):
    if split:
        return [pl.BlockSpec(shape, index)] * ranks
    return [pl.BlockSpec((ranks,) + shape, lambda *at: (0,) + index(*at))]


def each_slab(refs, ranks, me):
    if len(refs) == 1:
        return [(s, refs[0].at[s]) for s in range(ranks)]
    return [(s ^ me, refs[s]) for s in range(ranks)]


def unread(deps):
    return [pl.BlockSpec(memory_space=pl.ANY)] * len(deps)


def image_at(plan, len_ref, me_ref):
    c, chunks, images = plan
    if chunks != 2 or images != 1:
        return c * images
    swap = (len_ref[me_ref[2] + 1] < len_ref[me_ref[2]]).astype(jnp.int32)
    return 1 - swap if c else swap


def span(rank, size):
    if isinstance(rank, int):
        return pl.ds(rank * size, size)
    return pl.ds(pl.multiple_of(rank * size, size), size)


def pack_kernel(per, parts, _, __, *refs):
    ins, out = refs[:parts], refs[-1]
    for part in range(parts):
        for r in range(out.shape[0]):
            for j in range(per):
                at = (r * per + j) * HD
                out[r, part, j] = ins[part][0, :, at : at + HD]


def pack_slabs_kernel(per, parts, ranks, _, __, *refs):
    ins, outs = refs[: ranks * parts], refs[-ranks:]
    for s in range(ranks):
        for part in range(parts):
            for j in range(per):
                outs[s][part, j] = ins[s * parts + part][0, :, j * HD : (j + 1) * HD]


def pack(arrays, plan, ranks, per, split, where, deps):
    seg, width = arrays[0].shape[1:]
    parts, images = len(arrays), plan[2]
    ranks_image = ranks // images
    if split:
        steps = 2 if seg % 32 == 0 else 1
        rows = seg // steps

        def column(s):
            return pl.BlockSpec(
                (1, rows, per * HD),
                lambda h, n, m: (
                    image_at(plan, n, m) + lax.div(m[0] ^ s, ranks_image),
                    h,
                    lax.rem(m[0] ^ s, ranks_image),
                ),
            )

        kernel = functools.partial(pack_slabs_kernel, per, parts, ranks)
        operands = list(arrays) * ranks
        in_specs = [column(s) for s in range(ranks) for _ in range(parts)]
        out_specs = slab_specs(split, ranks, (parts, per, rows, HD), lambda h, n, m: (0, 0, h, 0))
    else:
        group = 2 if ranks_image % 2 == 0 else 1
        steps_image = ranks_image // group
        steps = ranks // group
        kernel = functools.partial(pack_kernel, per, parts)
        operands = list(arrays)
        in_specs = [
            pl.BlockSpec(
                (1, seg, group * per * HD),
                lambda s, n, m: (
                    image_at(plan, n, m) + lax.div(s, steps_image),
                    0,
                    lax.rem(s, steps_image),
                ),
            )
        ] * parts
        out_specs = [
            pl.BlockSpec((group, parts, per, seg, HD), lambda s, n, m: (s, 0, 0, 0, 0))
        ]
    return pl.pallas_call(
        kernel,
        grid_spec=pltpu.PrefetchScalarGridSpec(
            num_scalar_prefetch=2,
            grid=(steps,),
            in_specs=in_specs + unread(deps),
            out_specs=out_specs,
        ),
        out_shape=slab_shapes(split, ranks, (parts, per, seg, HD)),
        cost_estimate=cost(0, 4 * parts * images * seg * width),
        compiler_params=pltpu.CompilerParams(vmem_limit_bytes=VMEM_LIMIT),
        name="pack",
    )(*where, *operands, *deps)


def unpack_kernel(per, parts, _, __, *refs):
    src, outs = refs[0], refs[-parts:]
    for part in range(parts):
        for r in range(src.shape[0]):
            for j in range(per):
                at = (r * per + j) * HD
                outs[part][0, :, at : at + HD] = src[r, part, j]


def unpack(block, plan, count, where, held, deps):
    ranks, parts, per, seg, _ = block.shape
    images = plan[2]
    width = ranks * per // images * HD
    ranks_image = ranks // images
    group = 2 if ranks_image % 2 == 0 else 1
    steps_image = ranks_image // group
    held = list(held)

    def at(s, n, m):
        image = image_at(plan, n, m) + lax.div(s, steps_image)
        return image, 0, lax.rem(s, steps_image)

    return pl.pallas_call(
        functools.partial(unpack_kernel, per, parts),
        grid_spec=pltpu.PrefetchScalarGridSpec(
            num_scalar_prefetch=2,
            grid=(ranks // group,),
            in_specs=[
                pl.BlockSpec((group, parts, per, seg, HD), lambda s, n, m: (s, 0, 0, 0, 0))
            ]
            + unread(held)
            + unread(deps),
            out_specs=[pl.BlockSpec((1, seg, group * per * HD), at)] * parts,
        ),
        out_shape=[jax.ShapeDtypeStruct((count, seg, width), jnp.bfloat16)] * parts,
        input_output_aliases={3 + i: i for i in range(len(held))},
        cost_estimate=cost(0, 4 * parts * images * seg * width),
        compiler_params=pltpu.CompilerParams(vmem_limit_bytes=VMEM_LIMIT),
        name="unpack",
    )(*where, block, *held, *deps)


def place_kernel(per, parts, _, __, src, *refs):
    for part in range(parts):
        for j in range(per):
            refs[parts + part][0, :, j * HD : (j + 1) * HD] = src[part, j]


def place(slab, distance, plan, count, ranks, where, held):
    parts, per, seg, _ = slab.shape
    images = plan[2]
    width = ranks * per // images * HD
    ranks_image = ranks // images

    def at(s, n, m):
        owner = m[0] ^ distance
        image = image_at(plan, n, m) + lax.div(owner, ranks_image)
        return image, 0, lax.rem(owner, ranks_image)

    return pl.pallas_call(
        functools.partial(place_kernel, per, parts),
        grid_spec=pltpu.PrefetchScalarGridSpec(
            num_scalar_prefetch=2,
            grid=(1,),
            in_specs=[pl.BlockSpec((parts, per, seg, HD), lambda s, n, m: (0, 0, 0, 0))]
            + unread(held),
            out_specs=[pl.BlockSpec((1, seg, per * HD), at)] * parts,
        ),
        out_shape=[jax.ShapeDtypeStruct((count, seg, width), jnp.bfloat16)] * parts,
        input_output_aliases={3 + i: i for i in range(parts)},
        cost_estimate=cost(0, 4 * parts * per * seg * HD),
        compiler_params=pltpu.CompilerParams(vmem_limit_bytes=VMEM_LIMIT_PLACE),
        name="place",
    )(*where, slab, *held)


def tiles_of(total, seg):
    return min(total, max(512, seg)), min(total, max(512, seg))


def for_each_count(count, most, body):
    for n in range(1, most + 1):
        pl.when(count == n)(functools.partial(body, n))


def pair_length(len_ref, me_ref, plan, heads):
    pair = me_ref[0] * pl.num_programs(0) + pl.program_id(0)
    return len_ref[me_ref[2] + image_at(plan, len_ref, me_ref) + lax.div(pair, heads)]


def forward_kernel(sizes, len_ref, me_ref, *refs):
    n_slabs, n_deps, ranks, seg, tq, tk, plan, heads = sizes
    ins, refs = refs[:n_slabs], refs[n_slabs + n_deps :]
    outs = refs[:n_slabs]
    st_ref, ot_ref, q_ref, k_ref, v_ref, vt_ref, even_ref, odd_ref, o_ref = refs[n_slabs:]
    length = pair_length(len_ref, me_ref, plan, heads)
    total = ranks * seg
    for r, slab in each_slab(ins, ranks, me_ref[0]):
        rows = span(r, seg)
        q_ref[rows, :] = slab[0]
        k_ref[rows, :] = slab[1]
        v_ref[rows, :] = slab[2]
    for t in range(total // tk):
        vt_ref[:HD, t * tk : (t + 1) * tk] = v_ref[t * tk : (t + 1) * tk, :].T
    vt_ref[HD:, :] = jnp.ones_like(vt_ref[HD:, :])
    nq = lax.div(length + (tq - 1), tq)
    nk = lax.div(length + (tk - 1), tk)

    last_step = total // tq - 1

    def with_tiles(tiles):
        def scores(i, s_ref, t, top):
            rows = slice(t * tk, (t + 1) * tk)
            s = dot(k_ref[rows, :], q_ref[span(i, tq), :], NT)
            if t == tiles - 1:
                row = lax.broadcasted_iota(jnp.int32, (tk, tq), 0) + t * tk
                s = jnp.where(row < length, s, NEG)
            s_ref[rows, :] = s
            high = jnp.max(s, axis=0, keepdims=True)
            return high if top is None else jnp.maximum(top, high)

        def q_step(i, top, s_ref, next_ref):
            acc, next_top = jnp.zeros((vt_ref.shape[0], tq), jnp.float32), None
            for t in range(tiles):
                rows = slice(t * tk, (t + 1) * tk)
                next_top = scores(jnp.minimum(i + 1, last_step), next_ref, t, next_top)
                p = jnp.exp2((s_ref[rows, :] - top) * (SCALE * LOG2E))
                acc = acc + dot(vt_ref[:, rows], p.astype(jnp.bfloat16), NN)
            denom = acc[HD : HD + 1]
            out = acc[:HD] * (1.0 / denom)
            st_ref[0:1, span(i, tq)] = top * (SCALE * LOG2E) + jnp.log2(denom)
            ot_ref[:, span(i, tq)] = out
            o_ref[span(i, tq), :] = out.T.astype(jnp.bfloat16)
            return next_top

        def two_steps(pair, top):
            top = q_step(2 * pair, top, even_ref, odd_ref)
            if last_step == 0:
                return top
            return q_step(2 * pair + 1, top, odd_ref, even_ref)

        top = None
        for t in range(tiles):
            top = scores(0, even_ref, t, top)
        lax.fori_loop(0, lax.div(nq + 1, 2), two_steps, top)

    for_each_count(nk, total // tk, with_tiles)

    def blank(i, _):
        o_ref[span(i, tq), :] = jnp.zeros((tq, HD), jnp.bfloat16)
        return 0

    lax.fori_loop(nq, total // tq, blank, 0)
    for r, slab in each_slab(outs, ranks, me_ref[0]):
        slab[...] = o_ref[span(r, seg), :]


def forward(qkv, plan, ranks, where, deps):
    split = len(qkv) > 1
    per, seg = qkv[0].shape[-3:-1]
    heads = ranks * per // plan[2]
    total = ranks * seg
    tq, tk = tiles_of(total, seg)
    *attended, stats, kept = pl.pallas_call(
        functools.partial(forward_kernel, (len(qkv), len(deps), ranks, seg, tq, tk, plan, heads)),
        grid_spec=pltpu.PrefetchScalarGridSpec(
            num_scalar_prefetch=2,
            grid=(per,),
            in_specs=slab_specs(split, ranks, (3, None, seg, HD), lambda p, n, m: (0, p, 0, 0))
            + unread(deps),
            out_specs=slab_specs(split, ranks, (None, seg, HD), lambda p, n, m: (p, 0, 0))
            + [
                pl.BlockSpec((None, 8, total), lambda p, n, m: (p, 0, 0)),
                pl.BlockSpec((None, HD, total), lambda p, n, m: (p, 0, 0)),
            ],
            scratch_shapes=[pltpu.VMEM((total, HD), jnp.bfloat16)] * 3
            + [
                pltpu.VMEM((HD + 16, total), jnp.bfloat16),
                pltpu.VMEM((total, tq), jnp.float32),
                pltpu.VMEM((total, tq), jnp.float32),
                pltpu.VMEM((total, HD), jnp.bfloat16),
            ],
        ),
        out_shape=slab_shapes(split, ranks, (per, seg, HD))
        + [
            jax.ShapeDtypeStruct((per, 8, total), jnp.float32),
            jax.ShapeDtypeStruct((per, HD, total), jnp.float32),
        ],
        cost_estimate=cost(8 * per * total * total * HD, 8 * per * total * HD, per * total * total),
        compiler_params=pltpu.CompilerParams(vmem_limit_bytes=VMEM_LIMIT),
        name="attend_fwd",
    )(*where, *qkv, *deps)
    return attended, (stats, kept)


def weights_kernel(sizes, len_ref, me_ref, *refs):
    n_slabs, ranks, seg, tq, tk, plan, heads, per = sizes
    ins, st_ref, p_ref = refs[:n_slabs], refs[n_slabs], refs[n_slabs + 1]
    q_ref, k_ref = refs[n_slabs + 2 :]
    i = pl.program_id(1)
    pair = me_ref[0] * per + pl.program_id(0)
    length = len_ref[me_ref[2] + image_at(plan, len_ref, me_ref) + lax.div(pair, heads)]

    @pl.when(i == 0)
    def _():
        for r, slab in each_slab(ins, ranks, me_ref[0]):
            q_ref[span(r, seg), :] = slab[0]
            k_ref[span(r, seg), :] = slab[1]

    @pl.when(i * tq < length)
    def _():
        q = q_ref[span(i, tq), :]
        for t in range(ranks * seg // tk):
            rows = slice(t * tk, (t + 1) * tk)
            s = dot(k_ref[rows, :], q, NT) * (SCALE * LOG2E) - st_ref[0:1, :]
            row = lax.broadcasted_iota(jnp.int32, (tk, tq), 0) + t * tk
            p_ref[rows, :] = jnp.exp2(jnp.where(row < length, s, NEG)).astype(jnp.bfloat16)


def weights(qkv, stats, plan, ranks, where):
    split = len(qkv) > 1
    per, seg = qkv[0].shape[-3:-1]
    heads = ranks * per // plan[2]
    total = ranks * seg
    tq, tk = tiles_of(total, seg)
    return pl.pallas_call(
        functools.partial(weights_kernel, (len(qkv), ranks, seg, tq, tk, plan, heads, per)),
        grid_spec=pltpu.PrefetchScalarGridSpec(
            num_scalar_prefetch=2,
            grid=(per, total // tq),
            in_specs=slab_specs(split, ranks, (3, None, seg, HD), lambda p, i, n, m: (0, p, 0, 0))
            + [pl.BlockSpec((None, 8, tq), lambda p, i, n, m: (p, 0, i))],
            out_specs=pl.BlockSpec((None, total, tq), lambda p, i, n, m: (p, 0, i)),
            scratch_shapes=[pltpu.VMEM((total, HD), jnp.bfloat16)] * 2,
        ),
        out_shape=jax.ShapeDtypeStruct((per, total, total), jnp.bfloat16),
        cost_estimate=cost(2 * per * total * total * HD, 2 * per * total * total),
        compiler_params=pltpu.CompilerParams(vmem_limit_bytes=VMEM_LIMIT),
        name="weights",
    )(*where, *qkv, stats)


def backward_kernel(sizes, len_ref, me_ref, *refs):
    n_slabs, n_deps, n_weights, ranks, seg, tq, tk, plan, heads = sizes
    ins, g_ins = refs[:n_slabs], refs[n_slabs : 2 * n_slabs]
    n_kept = 3 if n_weights else 2
    st_ref, ot_ref, *w_ref = refs[2 * n_slabs : 2 * n_slabs + n_kept]
    refs = refs[2 * n_slabs + n_kept + n_deps :]
    outs = refs[:n_slabs]
    q_ref, k_ref, v_ref, g_ref, kt_ref, dq_ref, dk_ref, dv_ref, *buf = refs[n_slabs:]

    def fetch(i, slot):
        buf_ref, sems = buf
        source = w_ref[0].at[pl.program_id(0), :, span(i, tq)]
        return pltpu.make_async_copy(source, buf_ref.at[slot], sems.at[slot])

    if n_weights:
        fetch(0, 0).start()
    length = pair_length(len_ref, me_ref, plan, heads)
    total = ranks * seg
    for r, slab in each_slab(ins, ranks, me_ref[0]):
        rows = span(r, seg)
        q_ref[rows, :] = slab[0]
        k_ref[rows, :] = slab[1]
        v_ref[rows, :] = slab[2]
    for r, slab in each_slab(g_ins, ranks, me_ref[0]):
        g_ref[span(r, seg), :] = slab[...]
    for t in range(total // tk):
        kt_ref[:, t * tk : (t + 1) * tk] = k_ref[t * tk : (t + 1) * tk, :].T
    nq = lax.div(length + (tq - 1), tq)
    nk = lax.div(length + (tk - 1), tk)
    dk_ref[...] = jnp.zeros_like(dk_ref)
    dv_ref[...] = jnp.zeros_like(dv_ref)

    def with_tiles(tiles):
        def q_step(i, _):
            q = q_ref[span(i, tq), :]
            g = g_ref[span(i, tq), :]
            offset = st_ref[0:1, span(i, tq)]
            delta = jnp.sum(
                ot_ref[:, span(i, tq)] * g.astype(jnp.float32).T, axis=0, keepdims=True
            )
            dq = jnp.zeros((HD, tq), jnp.float32)

            part = tk // 2
            parts = [slice(at, at + part) for at in range(0, tiles * tk, part)]

            if n_weights:
                slot = lax.rem(i, 2)

                @pl.when(i + 1 < nq)
                def _():
                    fetch(i + 1, 1 - slot).start()

                fetch(i, slot).wait()

            def products(rows):
                dp = dot(v_ref[rows, :], g, NT)
                if n_weights:
                    return buf[0][slot, rows, :], dp
                return dot(k_ref[rows, :], q, NT), dp

            ahead = products(parts[0])
            for t, rows in enumerate(parts):
                s, dp = ahead
                if t + 1 < len(parts):
                    ahead = products(parts[t + 1])
                if n_weights:
                    p = s.astype(jnp.float32)
                else:
                    s = s * (SCALE * LOG2E) - offset
                    if t + 2 >= len(parts):
                        row = lax.broadcasted_iota(jnp.int32, (part, tq), 0) + rows.start
                        s = jnp.where(row < length, s, NEG)
                    p = jnp.exp2(s)
                ds = (p * (dp - delta)).astype(jnp.bfloat16)
                dv_ref[rows, :] += dot(p.astype(jnp.bfloat16), g, NN)
                dk_ref[rows, :] += dot(ds, q, NN)
                dq = dq + dot(kt_ref[:, rows], ds, NN)
            dq_ref[span(i, tq), :] = (dq.T * SCALE).astype(jnp.bfloat16)
            return 0

        lax.fori_loop(0, nq, q_step, 0)

    for_each_count(nk, total // tk, with_tiles)

    def blank(i, _):
        dq_ref[span(i, tq), :] = jnp.zeros((tq, HD), jnp.bfloat16)
        return 0

    lax.fori_loop(nq, total // tq, blank, 0)
    for r, slab in each_slab(outs, ranks, me_ref[0]):
        rows = span(r, seg)
        slab[0] = dq_ref[rows, :]
        slab[1] = (dk_ref[rows, :] * SCALE).astype(jnp.bfloat16)
        slab[2] = dv_ref[rows, :].astype(jnp.bfloat16)


def backward(qkv, g_in, kept, probs, plan, ranks, where, deps):
    split = len(qkv) > 1
    per, seg = qkv[0].shape[-3:-1]
    heads = ranks * per // plan[2]
    total = ranks * seg
    tq, tk = tiles_of(total, seg)
    block = (3, None, seg, HD)
    held = [] if probs is None else [probs]
    return pl.pallas_call(
        functools.partial(backward_kernel, (len(qkv), len(deps), len(held), ranks, seg, tq, tk, plan, heads)),
        grid_spec=pltpu.PrefetchScalarGridSpec(
            num_scalar_prefetch=2,
            grid=(per,),
            in_specs=slab_specs(split, ranks, block, lambda p, n, m: (0, p, 0, 0))
            + slab_specs(split, ranks, (None, seg, HD), lambda p, n, m: (p, 0, 0))
            + [
                pl.BlockSpec((None, 8, total), lambda p, n, m: (p, 0, 0)),
                pl.BlockSpec((None, HD, total), lambda p, n, m: (p, 0, 0)),
            ]
            + unread(held)
            + unread(deps),
            out_specs=slab_specs(split, ranks, block, lambda p, n, m: (0, p, 0, 0)),
            scratch_shapes=[pltpu.VMEM((total, HD), jnp.bfloat16)] * 4
            + [
                pltpu.VMEM((HD, total), jnp.bfloat16),
                pltpu.VMEM((total, HD), jnp.bfloat16),
                pltpu.VMEM((total, HD), jnp.float32),
                pltpu.VMEM((total, HD), jnp.float32),
            ]
            + [pltpu.VMEM((2, total, tq), jnp.bfloat16), pltpu.SemaphoreType.DMA((2,))] * len(held),
        ),
        out_shape=slab_shapes(split, ranks, (3, per, seg, HD)),
        cost_estimate=cost(20 * per * total * total * HD, 14 * per * total * HD, per * total * total),
        compiler_params=pltpu.CompilerParams(vmem_limit_bytes=VMEM_LIMIT),
        name="attend_bwd",
    )(*where, *qkv, *g_in, *kept, *held, *deps)


def gather_rows(rows, deps):
    planes = lax.axis_size("grp") * lax.axis_size("dp")
    enc = rows.shape[1]
    shares = 1
    while shares * 2 <= planes and enc % (shares * 2 * HD) == 0:
        shares *= 2
    plane = lax.axis_index("grp") * lax.axis_size("dp") + lax.axis_index("dp")
    wide = enc // shares
    mine = lax.dynamic_slice_in_dim(rows, (plane % shares) * wide, wide, axis=1)
    along = after(lax.all_gather(mine, "seq", axis=0, tiled=True), deps)
    groups = [list(range(at, at + shares)) for at in range(0, planes, shares)]
    return lax.all_gather(
        along, ("grp", "dp"), axis=0, axis_index_groups=groups if len(groups) > 1 else None
    )


def norm_kernel(t_ref, gain_ref, bias_ref, _, out_ref):
    data = t_ref[...].astype(jnp.float32)
    center = data - jnp.mean(data, axis=-1, keepdims=True)
    spread = jnp.mean(center * center, axis=-1, keepdims=True)
    normed = center * lax.rsqrt(spread + EPS) * gain_ref[...] + bias_ref[...]
    out_ref[...] = normed.astype(jnp.bfloat16)


def layer_norm(rows, gain, bias, dep):
    count, seg, enc = rows.shape
    block = pl.BlockSpec((None, seg, enc), lambda b: (b, 0, 0))
    vector = pl.BlockSpec((1, enc), lambda b: (0, 0))
    return pl.pallas_call(
        norm_kernel,
        grid=(count,),
        in_specs=[block, vector, vector] + unread([dep]),
        out_specs=block,
        out_shape=jax.ShapeDtypeStruct(rows.shape, jnp.bfloat16),
        cost_estimate=cost(10 * rows.size, 4 * rows.size),
        compiler_params=pltpu.CompilerParams(vmem_limit_bytes=VMEM_LIMIT),
        name="layer_norm",
    )(rows, gain.reshape(1, -1), bias.reshape(1, -1), dep)


def after_kernel(*_):
    pass


def after(value, deps):
    return pl.pallas_call(
        after_kernel,
        in_specs=unread([value, *deps]),
        out_specs=pl.BlockSpec(memory_space=pl.ANY),
        out_shape=jax.ShapeDtypeStruct(value.shape, value.dtype),
        input_output_aliases={0: 0},
        cost_estimate=cost(0, 0),
        name="after",
    )(value, *deps)


def head_kernel(sizes, len_ref, me_ref, *refs):
    n_slabs, ranks, plan, per, seg = sizes
    images = plan[2]
    image = image_at(plan, len_ref, me_ref)
    ins = refs[:n_slabs]
    w_ref, t_ref = refs[n_slabs : n_slabs + 2]
    outs, rows_ref = refs[-1 - n_slabs : -1], refs[-1]
    heads = ranks * per // images

    def place_of(r, j):
        pair = r * per + j
        return span(lax.div(pair, heads), seg), span(lax.rem(pair, heads), HD)

    for r, slab in each_slab(ins, ranks, me_ref[0]):
        for j in range(per):
            rows, cols = place_of(jnp.int32(r), j)
            rows_ref[rows, cols] = slab[j]
    shares, _, wide = w_ref.shape
    for b in range(images):
        rows = rows_ref[b * seg : (b + 1) * seg, :]
        aligned = jnp.concatenate([dot(rows, w_ref[part], NN) for part in range(shares)], axis=1)
        tgt = t_ref[b].astype(jnp.float32)
        width = aligned.shape[-1]
        inner = jnp.mean(aligned * tgt, axis=-1, keepdims=True)
        own = jnp.mean(aligned * aligned, axis=-1, keepdims=True) + EPS
        other = jnp.mean(tgt * tgt, axis=-1, keepdims=True) + EPS
        inverse = lax.rsqrt(own * other)
        cosine = inner * inverse
        row = lax.broadcasted_iota(jnp.int32, (seg, 1), 0) + me_ref[1]
        keep = jnp.where(row < len_ref[me_ref[2] + image + b], -COEF / width, 0.0)
        grad = (keep * (tgt * inverse - cosine / own * aligned)).astype(jnp.bfloat16)
        grad_rows = dot(grad[:, :wide], w_ref[0], NT)
        for part in range(1, shares):
            grad_rows += dot(grad[:, part * wide : (part + 1) * wide], w_ref[part], NT)
        rows_ref[b * seg : (b + 1) * seg, :] = grad_rows.astype(jnp.bfloat16)
    for r, slab in each_slab(outs, ranks, me_ref[0]):
        for j in range(per):
            rows, cols = place_of(jnp.int32(r), j)
            slab[j] = rows_ref[rows, cols]


def align_head(back, whole, target, plan, ranks, where, deps):
    split = len(back) > 1
    per, seg = back[0].shape[-3:-1]
    shares, width, wide = whole.shape
    enc, images = shares * wide, plan[2]
    slabs = slab_specs(split, ranks, (per, seg, HD), lambda b, n, m: (0, 0, 0))
    return pl.pallas_call(
        functools.partial(head_kernel, (len(back), ranks, plan, per, seg)),
        grid_spec=pltpu.PrefetchScalarGridSpec(
            num_scalar_prefetch=2,
            grid=(1,),
            in_specs=slabs
            + [
                pl.BlockSpec((shares, width, wide), lambda b, n, m: (0, 0, 0)),
                pl.BlockSpec((images, seg, enc), lambda b, n, m: (lax.div(image_at(plan, n, m), images), 0, 0)),
            ]
            + unread(deps),
            out_specs=slabs,
            scratch_shapes=[pltpu.VMEM((images * seg, width), jnp.bfloat16)],
        ),
        out_shape=slab_shapes(split, ranks, (per, seg, HD)),
        cost_estimate=cost(
            4 * images * seg * width * enc, 2 * width * enc + 10 * images * seg * width, 0
        ),
        compiler_params=pltpu.CompilerParams(vmem_limit_bytes=VMEM_LIMIT),
        name="align_head",
    )(*where, *back, whole, target, *deps)


def shards(queries, key_states, value_states, projector, teacher, enc_gain, enc_bias, valid_len):
    ranks = lax.axis_size("seq")
    count, seg, width = queries.shape
    heads = width // HD
    images = 1
    while images * heads % ranks:
        images *= 2
    chunks = count // images
    per = images * heads // ranks
    rank = lax.axis_index("seq").astype(jnp.int32)

    first_image = (lax.axis_index("grp") * lax.axis_size("dp") + lax.axis_index("dp")) * count
    where = (valid_len, jnp.stack([rank, rank * seg, first_image.astype(jnp.int32)]))
    plans = [(c, chunks, images) for c in range(chunks)]
    split = [chunks > 1 and c == chunks - 1 for c in range(chunks)]

    arrays = (queries, key_states, value_states)
    packed = []
    for c in range(chunks):
        deps = [slabs[0] for slabs in packed]
        packed.append(pack(arrays, plans[c], ranks, per, split[c], where, deps))
    normed = layer_norm(teacher, enc_gain, enc_bias, packed[0][0])
    target = from_partner(normed, "grp", 0)
    whole = gather_rows(projector, packed[-1][:1])

    def ahead(near, made, c, also=[]):
        if not split[-1]:
            return []
        return made[c - 1][:1] if split[c] else near[-1][:3] + also

    qkv = [exchange(slabs) for slabs in packed]
    attended, kept = [], []
    probs = [None] * chunks
    for c in range(chunks):
        deps = ahead(qkv, attended, c, [target])
        if c and split[c]:
            probs[c - 1] = weights(qkv[c - 1], kept[c - 1][0], plans[c - 1], ranks, where)
            deps = list(deps) + [probs[c - 1]]
        slabs, state = forward(qkv[c], plans[c], ranks, where, deps)
        kept.append(state)
        attended.append(slabs)
    back = [exchange(slabs) for slabs in attended]
    grad_rows = []
    for c in range(chunks):
        deps = ahead(back, grad_rows, c)
        grad_rows.append(align_head(back[c], whole, target, plans[c], ranks, where, deps))
    g_in = [exchange(slabs) for slabs in grad_rows]
    grads = []
    for c in range(chunks):
        deps = ahead(g_in, grads, c)
        grads.append(backward(qkv[c], g_in[c], kept[c], probs[c], plans[c], ranks, where, deps))
    grads = [exchange(slabs) for slabs in grads]
    outs = ()
    for c in range(chunks):
        if not split[c]:
            outs = unpack(grads[c][0], plans[c], count, where, outs, ahead(grads, None, c))
            continue
        for s, slab in enumerate(grads[c]):
            outs = place(slab, s, plans[c], count, ranks, where, outs)
    return tuple(outs)


def solution(mesh):
    return jax.shard_map(
        shards,
        mesh=mesh,
        in_specs=(
            P(("grp", "dp"), "seq", None),
            P(("grp", "dp"), "seq", None),
            P(("grp", "dp"), "seq", None),
            P("seq", None),
            P(("grp", "dp"), "seq", None),
            P(),
            P(),
            P(),
        ),
        out_specs=(
            P(("grp", "dp"), "seq", None),
            P(("grp", "dp"), "seq", None),
            P(("grp", "dp"), "seq", None),
        ),
        check_vma=False,
    )
```

```python
import functools

import jax
import jax.numpy as jnp
from jax import lax
from jax.experimental import pallas as pl
from jax.experimental.pallas import tpu as pltpu
from jax.sharding import PartitionSpec as P

HD = 128
EPS = 1e-06
COEF = 2048.0
SCALE = HD ** (-0.5)
LOG2E = 1.4426950408889634
NEG = -1e30
NT = (((1,), (1,)), ((), ()))
NN = (((1,), (0,)), ((), ()))
TN = (((0,), (0,)), ((), ()))
VMEM_LIMIT = 62 * 1024 * 1024
VMEM_LIMIT_PLACE = 16 * 1024 * 1024
WEIGHT = 16


def dot(a, b, dims):
    return lax.dot_general(a, b, dims, preferred_element_type=jnp.float32)


def cost(flops, data, exps=0):
    return pl.CostEstimate(
        flops=WEIGHT * flops, bytes_accessed=WEIGHT * data, transcendentals=WEIGHT * exps
    )


def from_partner(value, axis, apart):
    return lax.ppermute(value, axis, [(i, i ^ 1 << apart) for i in range(lax.axis_size(axis))])


def exchange(slabs):
    if len(slabs) == 1:
        return [lax.all_to_all(slabs[0], "seq", split_axis=0, concat_axis=0, tiled=True)]
    ranks = len(slabs)
    return [
        lax.ppermute(slab, "seq", [(i, i ^ s) for i in range(ranks)]) if s else slab
        for s, slab in enumerate(slabs)
    ]


def slab_shapes(split, ranks, shape, dtype=jnp.bfloat16):
    if split:
        return [jax.ShapeDtypeStruct(shape, dtype)] * ranks
    return [jax.ShapeDtypeStruct((ranks,) + shape, dtype)]


def slab_specs(split, ranks, shape, index):
    if split:
        return [pl.BlockSpec(shape, index)] * ranks
    return [pl.BlockSpec((ranks,) + shape, lambda *at: (0,) + index(*at))]


def each_slab(refs, ranks, me):
    if len(refs) == 1:
        return [(s, refs[0].at[s]) for s in range(ranks)]
    return [(s ^ me, refs[s]) for s in range(ranks)]


def unread(deps):
    return [pl.BlockSpec(memory_space=pl.ANY)] * len(deps)


def image_at(plan, len_ref, me_ref):
    c, chunks, images = plan
    if chunks != 2 or images != 1:
        return c * images
    swap = (len_ref[me_ref[2] + 1] < len_ref[me_ref[2]]).astype(jnp.int32)
    return 1 - swap if c else swap


def span(rank, size):
    if isinstance(rank, int):
        return pl.ds(rank * size, size)
    return pl.ds(pl.multiple_of(rank * size, size), size)


def pack_kernel(per, parts, _, __, *refs):
    ins, out = refs[:parts], refs[-1]
    for part in range(parts):
        for r in range(out.shape[0]):
            for j in range(per):
                at = (r * per + j) * HD
                out[r, part, j] = ins[part][0, :, at : at + HD]


def pack_slabs_kernel(per, parts, ranks, _, __, *refs):
    ins, outs = refs[: ranks * parts], refs[-ranks:]
    for s in range(ranks):
        for part in range(parts):
            for j in range(per):
                outs[s][part, j] = ins[s * parts + part][0, :, j * HD : (j + 1) * HD]


def pack(arrays, plan, ranks, per, split, where, deps):
    seg, width = arrays[0].shape[1:]
    parts, images = len(arrays), plan[2]
    ranks_image = ranks // images
    if split:
        steps = 2 if seg % 32 == 0 else 1
        rows = seg // steps

        def column(s):
            return pl.BlockSpec(
                (1, rows, per * HD),
                lambda h, n, m: (
                    image_at(plan, n, m) + lax.div(m[0] ^ s, ranks_image),
                    h,
                    lax.rem(m[0] ^ s, ranks_image),
                ),
            )

        kernel = functools.partial(pack_slabs_kernel, per, parts, ranks)
        operands = list(arrays) * ranks
        in_specs = [column(s) for s in range(ranks) for _ in range(parts)]
        out_specs = slab_specs(split, ranks, (parts, per, rows, HD), lambda h, n, m: (0, 0, h, 0))
    else:
        group = 2 if ranks_image % 2 == 0 else 1
        steps_image = ranks_image // group
        steps = ranks // group
        kernel = functools.partial(pack_kernel, per, parts)
        operands = list(arrays)
        in_specs = [
            pl.BlockSpec(
                (1, seg, group * per * HD),
                lambda s, n, m: (
                    image_at(plan, n, m) + lax.div(s, steps_image),
                    0,
                    lax.rem(s, steps_image),
                ),
            )
        ] * parts
        out_specs = [
            pl.BlockSpec((group, parts, per, seg, HD), lambda s, n, m: (s, 0, 0, 0, 0))
        ]
    return pl.pallas_call(
        kernel,
        grid_spec=pltpu.PrefetchScalarGridSpec(
            num_scalar_prefetch=2,
            grid=(steps,),
            in_specs=in_specs + unread(deps),
            out_specs=out_specs,
        ),
        out_shape=slab_shapes(split, ranks, (parts, per, seg, HD)),
        cost_estimate=cost(0, 4 * parts * images * seg * width),
        compiler_params=pltpu.CompilerParams(vmem_limit_bytes=VMEM_LIMIT),
        name="pack",
    )(*where, *operands, *deps)


def unpack_kernel(per, parts, _, __, *refs):
    src, outs = refs[0], refs[-parts:]
    for part in range(parts):
        for r in range(src.shape[0]):
            for j in range(per):
                at = (r * per + j) * HD
                outs[part][0, :, at : at + HD] = src[r, part, j]


def unpack(block, plan, count, where, held, deps):
    ranks, parts, per, seg, _ = block.shape
    images = plan[2]
    width = ranks * per // images * HD
    ranks_image = ranks // images
    group = 2 if ranks_image % 2 == 0 else 1
    steps_image = ranks_image // group
    held = list(held)

    def at(s, n, m):
        image = image_at(plan, n, m) + lax.div(s, steps_image)
        return image, 0, lax.rem(s, steps_image)

    return pl.pallas_call(
        functools.partial(unpack_kernel, per, parts),
        grid_spec=pltpu.PrefetchScalarGridSpec(
            num_scalar_prefetch=2,
            grid=(ranks // group,),
            in_specs=[
                pl.BlockSpec((group, parts, per, seg, HD), lambda s, n, m: (s, 0, 0, 0, 0))
            ]
            + unread(held)
            + unread(deps),
            out_specs=[pl.BlockSpec((1, seg, group * per * HD), at)] * parts,
        ),
        out_shape=[jax.ShapeDtypeStruct((count, seg, width), jnp.bfloat16)] * parts,
        input_output_aliases={3 + i: i for i in range(len(held))},
        cost_estimate=cost(0, 4 * parts * images * seg * width),
        compiler_params=pltpu.CompilerParams(vmem_limit_bytes=VMEM_LIMIT),
        name="unpack",
    )(*where, block, *held, *deps)


def place_kernel(per, parts, _, __, src, *refs):
    for part in range(parts):
        for j in range(per):
            refs[parts + part][0, :, j * HD : (j + 1) * HD] = src[part, j]


def place(slab, distance, plan, count, ranks, where, held):
    parts, per, seg, _ = slab.shape
    images = plan[2]
    width = ranks * per // images * HD
    ranks_image = ranks // images

    def at(s, n, m):
        owner = m[0] ^ distance
        image = image_at(plan, n, m) + lax.div(owner, ranks_image)
        return image, 0, lax.rem(owner, ranks_image)

    return pl.pallas_call(
        functools.partial(place_kernel, per, parts),
        grid_spec=pltpu.PrefetchScalarGridSpec(
            num_scalar_prefetch=2,
            grid=(1,),
            in_specs=[pl.BlockSpec((parts, per, seg, HD), lambda s, n, m: (0, 0, 0, 0))]
            + unread(held),
            out_specs=[pl.BlockSpec((1, seg, per * HD), at)] * parts,
        ),
        out_shape=[jax.ShapeDtypeStruct((count, seg, width), jnp.bfloat16)] * parts,
        input_output_aliases={3 + i: i for i in range(parts)},
        cost_estimate=cost(0, 4 * parts * per * seg * HD),
        compiler_params=pltpu.CompilerParams(vmem_limit_bytes=VMEM_LIMIT_PLACE),
        name="place",
    )(*where, slab, *held)


def tiles_of(total, seg):
    return min(total, max(512, seg)), min(total, max(512, seg))


def for_each_count(count, most, body):
    for n in range(1, most + 1):
        pl.when(count == n)(functools.partial(body, n))


def pair_length(len_ref, me_ref, plan, heads):
    pair = me_ref[0] * pl.num_programs(0) + pl.program_id(0)
    return len_ref[me_ref[2] + image_at(plan, len_ref, me_ref) + lax.div(pair, heads)]


def forward_kernel(sizes, len_ref, me_ref, *refs):
    n_slabs, n_deps, ranks, seg, tq, tk, plan, heads = sizes
    ins, refs = refs[:n_slabs], refs[n_slabs + n_deps :]
    outs = refs[:n_slabs]
    st_ref, ot_ref, q_ref, k_ref, v_ref, vt_ref, even_ref, odd_ref, o_ref = refs[n_slabs:]
    length = pair_length(len_ref, me_ref, plan, heads)
    total = ranks * seg
    for r, slab in each_slab(ins, ranks, me_ref[0]):
        rows = span(r, seg)
        q_ref[rows, :] = slab[0]
        k_ref[rows, :] = slab[1]
        v_ref[rows, :] = slab[2]
    for t in range(total // tk):
        vt_ref[:HD, t * tk : (t + 1) * tk] = v_ref[t * tk : (t + 1) * tk, :].T
    vt_ref[HD:, :] = jnp.ones_like(vt_ref[HD:, :])
    nq = lax.div(length + (tq - 1), tq)
    nk = lax.div(length + (tk - 1), tk)

    last_step = total // tq - 1

    def with_tiles(tiles):
        def scores(i, s_ref, t, top):
            rows = slice(t * tk, (t + 1) * tk)
            s = dot(k_ref[rows, :], q_ref[span(i, tq), :], NT)
            if t == tiles - 1:
                row = lax.broadcasted_iota(jnp.int32, (tk, tq), 0) + t * tk
                s = jnp.where(row < length, s, NEG)
            s_ref[rows, :] = s
            high = jnp.max(s, axis=0, keepdims=True)
            return high if top is None else jnp.maximum(top, high)

        def q_step(i, top, s_ref, next_ref):
            acc, next_top = jnp.zeros((vt_ref.shape[0], tq), jnp.float32), None
            for t in range(tiles):
                rows = slice(t * tk, (t + 1) * tk)
                next_top = scores(jnp.minimum(i + 1, last_step), next_ref, t, next_top)
                p = jnp.exp2((s_ref[rows, :] - top) * (SCALE * LOG2E))
                acc = acc + dot(vt_ref[:, rows], p.astype(jnp.bfloat16), NN)
            denom = acc[HD : HD + 1]
            out = acc[:HD] * (1.0 / denom)
            st_ref[0:1, span(i, tq)] = top * (SCALE * LOG2E) + jnp.log2(denom)
            ot_ref[:, span(i, tq)] = out
            o_ref[span(i, tq), :] = out.T.astype(jnp.bfloat16)
            return next_top

        def two_steps(pair, top):
            top = q_step(2 * pair, top, even_ref, odd_ref)
            if last_step == 0:
                return top
            return q_step(2 * pair + 1, top, odd_ref, even_ref)

        top = None
        for t in range(tiles):
            top = scores(0, even_ref, t, top)
        lax.fori_loop(0, lax.div(nq + 1, 2), two_steps, top)

    for_each_count(nk, total // tk, with_tiles)

    def blank(i, _):
        o_ref[span(i, tq), :] = jnp.zeros((tq, HD), jnp.bfloat16)
        return 0

    lax.fori_loop(nq, total // tq, blank, 0)
    for r, slab in each_slab(outs, ranks, me_ref[0]):
        slab[...] = o_ref[span(r, seg), :]


def forward(qkv, plan, ranks, where, deps):
    split = len(qkv) > 1
    per, seg = qkv[0].shape[-3:-1]
    heads = ranks * per // plan[2]
    total = ranks * seg
    tq, tk = tiles_of(total, seg)
    *attended, stats, kept = pl.pallas_call(
        functools.partial(forward_kernel, (len(qkv), len(deps), ranks, seg, tq, tk, plan, heads)),
        grid_spec=pltpu.PrefetchScalarGridSpec(
            num_scalar_prefetch=2,
            grid=(per,),
            in_specs=slab_specs(split, ranks, (3, None, seg, HD), lambda p, n, m: (0, p, 0, 0))
            + unread(deps),
            out_specs=slab_specs(split, ranks, (None, seg, HD), lambda p, n, m: (p, 0, 0))
            + [
                pl.BlockSpec((None, 8, total), lambda p, n, m: (p, 0, 0)),
                pl.BlockSpec((None, HD, total), lambda p, n, m: (p, 0, 0)),
            ],
            scratch_shapes=[pltpu.VMEM((total, HD), jnp.bfloat16)] * 3
            + [
                pltpu.VMEM((HD + 16, total), jnp.bfloat16),
                pltpu.VMEM((total, tq), jnp.float32),
                pltpu.VMEM((total, tq), jnp.float32),
                pltpu.VMEM((total, HD), jnp.bfloat16),
            ],
        ),
        out_shape=slab_shapes(split, ranks, (per, seg, HD))
        + [
            jax.ShapeDtypeStruct((per, 8, total), jnp.float32),
            jax.ShapeDtypeStruct((per, HD, total), jnp.float32),
        ],
        cost_estimate=cost(8 * per * total * total * HD, 8 * per * total * HD, per * total * total),
        compiler_params=pltpu.CompilerParams(vmem_limit_bytes=VMEM_LIMIT),
        name="attend_fwd",
    )(*where, *qkv, *deps)
    return attended, (stats, kept)


def backward_kernel(sizes, len_ref, me_ref, *refs):
    n_slabs, n_deps, ranks, seg, tq, tk, plan, heads = sizes
    ins, g_ins = refs[:n_slabs], refs[n_slabs : 2 * n_slabs]
    st_ref, ot_ref = refs[2 * n_slabs : 2 * n_slabs + 2]
    refs = refs[2 * n_slabs + 2 + n_deps :]
    outs = refs[:n_slabs]
    q_ref, k_ref, v_ref, g_ref, dq_ref, dk_ref, dv_ref = refs[n_slabs:]
    length = pair_length(len_ref, me_ref, plan, heads)
    total = ranks * seg
    for r, slab in each_slab(ins, ranks, me_ref[0]):
        rows = span(r, seg)
        q_ref[rows, :] = slab[0]
        k_ref[rows, :] = slab[1]
        v_ref[rows, :] = slab[2]
    for r, slab in each_slab(g_ins, ranks, me_ref[0]):
        g_ref[span(r, seg), :] = slab[...]
    nq = lax.div(length + (tq - 1), tq)
    nk = lax.div(length + (tk - 1), tk)
    dk_ref[...] = jnp.zeros_like(dk_ref)
    dv_ref[...] = jnp.zeros_like(dv_ref)

    def with_tiles(tiles):
        def q_step(i, _):
            q = q_ref[span(i, tq), :]
            g = g_ref[span(i, tq), :]
            offset = st_ref[0:1, span(i, tq)]
            delta = jnp.sum(
                ot_ref[:, span(i, tq)] * g.astype(jnp.float32).T, axis=0, keepdims=True
            )
            dq = jnp.zeros((tq, HD), jnp.float32)

            part = tk // 2
            parts = [slice(at, at + part) for at in range(0, tiles * tk, part)]

            def products(rows):
                return dot(k_ref[rows, :], q, NT), dot(v_ref[rows, :], g, NT)

            ahead = products(parts[0])
            for t, rows in enumerate(parts):
                s, dp = ahead
                if t + 1 < len(parts):
                    ahead = products(parts[t + 1])
                s = s * (SCALE * LOG2E) - offset
                if t + 2 >= len(parts):
                    row = lax.broadcasted_iota(jnp.int32, (part, tq), 0) + rows.start
                    s = jnp.where(row < length, s, NEG)
                p = jnp.exp2(s)
                ds = (p * (dp - delta)).astype(jnp.bfloat16)
                dv_ref[rows, :] += dot(p.astype(jnp.bfloat16), g, NN)
                dk_ref[rows, :] += dot(ds, q, NN)
                dq = dq + dot(ds, k_ref[rows, :], TN)
            dq_ref[span(i, tq), :] = (dq * SCALE).astype(jnp.bfloat16)
            return 0

        lax.fori_loop(0, nq, q_step, 0)

    for_each_count(nk, total // tk, with_tiles)

    def blank(i, _):
        dq_ref[span(i, tq), :] = jnp.zeros((tq, HD), jnp.bfloat16)
        return 0

    lax.fori_loop(nq, total // tq, blank, 0)
    for r, slab in each_slab(outs, ranks, me_ref[0]):
        rows = span(r, seg)
        slab[0] = dq_ref[rows, :]
        slab[1] = (dk_ref[rows, :] * SCALE).astype(jnp.bfloat16)
        slab[2] = dv_ref[rows, :].astype(jnp.bfloat16)


def backward(qkv, g_in, kept, plan, ranks, where, deps):
    split = len(qkv) > 1
    per, seg = qkv[0].shape[-3:-1]
    heads = ranks * per // plan[2]
    total = ranks * seg
    tq, tk = tiles_of(total, seg)
    block = (3, None, seg, HD)
    return pl.pallas_call(
        functools.partial(backward_kernel, (len(qkv), len(deps), ranks, seg, tq, tk, plan, heads)),
        grid_spec=pltpu.PrefetchScalarGridSpec(
            num_scalar_prefetch=2,
            grid=(per,),
            in_specs=slab_specs(split, ranks, block, lambda p, n, m: (0, p, 0, 0))
            + slab_specs(split, ranks, (None, seg, HD), lambda p, n, m: (p, 0, 0))
            + [
                pl.BlockSpec((None, 8, total), lambda p, n, m: (p, 0, 0)),
                pl.BlockSpec((None, HD, total), lambda p, n, m: (p, 0, 0)),
            ]
            + unread(deps),
            out_specs=slab_specs(split, ranks, block, lambda p, n, m: (0, p, 0, 0)),
            scratch_shapes=[pltpu.VMEM((total, HD), jnp.bfloat16)] * 4
            + [
                pltpu.VMEM((total, HD), jnp.bfloat16),
                pltpu.VMEM((total, HD), jnp.float32),
                pltpu.VMEM((total, HD), jnp.float32),
            ],
        ),
        out_shape=slab_shapes(split, ranks, (3, per, seg, HD)),
        cost_estimate=cost(20 * per * total * total * HD, 14 * per * total * HD, per * total * total),
        compiler_params=pltpu.CompilerParams(vmem_limit_bytes=VMEM_LIMIT),
        name="attend_bwd",
    )(*where, *qkv, *g_in, *kept, *deps)


def gather_rows(rows, deps):
    planes = lax.axis_size("grp") * lax.axis_size("dp")
    enc = rows.shape[1]
    shares = 1
    while shares * 2 <= planes and enc % (shares * 2 * HD) == 0:
        shares *= 2
    plane = lax.axis_index("grp") * lax.axis_size("dp") + lax.axis_index("dp")
    wide = enc // shares
    mine = lax.dynamic_slice_in_dim(rows, (plane % shares) * wide, wide, axis=1)
    along = after(lax.all_gather(mine, "seq", axis=0, tiled=True), deps)
    groups = [list(range(at, at + shares)) for at in range(0, planes, shares)]
    return lax.all_gather(
        along, ("grp", "dp"), axis=0, axis_index_groups=groups if len(groups) > 1 else None
    )


def norm_kernel(t_ref, gain_ref, bias_ref, _, out_ref):
    data = t_ref[...].astype(jnp.float32)
    center = data - jnp.mean(data, axis=-1, keepdims=True)
    spread = jnp.mean(center * center, axis=-1, keepdims=True)
    normed = center * lax.rsqrt(spread + EPS) * gain_ref[...] + bias_ref[...]
    out_ref[...] = normed.astype(jnp.bfloat16)


def layer_norm(rows, gain, bias, dep):
    count, seg, enc = rows.shape
    block = pl.BlockSpec((None, seg, enc), lambda b: (b, 0, 0))
    vector = pl.BlockSpec((1, enc), lambda b: (0, 0))
    return pl.pallas_call(
        norm_kernel,
        grid=(count,),
        in_specs=[block, vector, vector] + unread([dep]),
        out_specs=block,
        out_shape=jax.ShapeDtypeStruct(rows.shape, jnp.bfloat16),
        cost_estimate=cost(10 * rows.size, 4 * rows.size),
        compiler_params=pltpu.CompilerParams(vmem_limit_bytes=VMEM_LIMIT),
        name="layer_norm",
    )(rows, gain.reshape(1, -1), bias.reshape(1, -1), dep)


def after_kernel(*_):
    pass


def after(value, deps):
    return pl.pallas_call(
        after_kernel,
        in_specs=unread([value, *deps]),
        out_specs=pl.BlockSpec(memory_space=pl.ANY),
        out_shape=jax.ShapeDtypeStruct(value.shape, value.dtype),
        input_output_aliases={0: 0},
        cost_estimate=cost(0, 0),
        name="after",
    )(value, *deps)


def head_kernel(sizes, len_ref, me_ref, *refs):
    n_slabs, ranks, plan, per, seg = sizes
    images = plan[2]
    image = image_at(plan, len_ref, me_ref)
    ins = refs[:n_slabs]
    w_ref, t_ref = refs[n_slabs : n_slabs + 2]
    outs, rows_ref = refs[-1 - n_slabs : -1], refs[-1]
    heads = ranks * per // images

    def place_of(r, j):
        pair = r * per + j
        return span(lax.div(pair, heads), seg), span(lax.rem(pair, heads), HD)

    for r, slab in each_slab(ins, ranks, me_ref[0]):
        for j in range(per):
            rows, cols = place_of(jnp.int32(r), j)
            rows_ref[rows, cols] = slab[j]
    shares, _, wide = w_ref.shape
    for b in range(images):
        rows = rows_ref[b * seg : (b + 1) * seg, :]
        aligned = jnp.concatenate([dot(rows, w_ref[part], NN) for part in range(shares)], axis=1)
        tgt = t_ref[b].astype(jnp.float32)
        width = aligned.shape[-1]
        inner = jnp.mean(aligned * tgt, axis=-1, keepdims=True)
        own = jnp.mean(aligned * aligned, axis=-1, keepdims=True) + EPS
        other = jnp.mean(tgt * tgt, axis=-1, keepdims=True) + EPS
        inverse = lax.rsqrt(own * other)
        cosine = inner * inverse
        row = lax.broadcasted_iota(jnp.int32, (seg, 1), 0) + me_ref[1]
        keep = jnp.where(row < len_ref[me_ref[2] + image + b], -COEF / width, 0.0)
        grad = (keep * (tgt * inverse - cosine / own * aligned)).astype(jnp.bfloat16)
        grad_rows = dot(grad[:, :wide], w_ref[0], NT)
        for part in range(1, shares):
            grad_rows += dot(grad[:, part * wide : (part + 1) * wide], w_ref[part], NT)
        rows_ref[b * seg : (b + 1) * seg, :] = grad_rows.astype(jnp.bfloat16)
    for r, slab in each_slab(outs, ranks, me_ref[0]):
        for j in range(per):
            rows, cols = place_of(jnp.int32(r), j)
            slab[j] = rows_ref[rows, cols]


def align_head(back, whole, target, plan, ranks, where, deps):
    split = len(back) > 1
    per, seg = back[0].shape[-3:-1]
    shares, width, wide = whole.shape
    enc, images = shares * wide, plan[2]
    slabs = slab_specs(split, ranks, (per, seg, HD), lambda b, n, m: (0, 0, 0))
    return pl.pallas_call(
        functools.partial(head_kernel, (len(back), ranks, plan, per, seg)),
        grid_spec=pltpu.PrefetchScalarGridSpec(
            num_scalar_prefetch=2,
            grid=(1,),
            in_specs=slabs
            + [
                pl.BlockSpec((shares, width, wide), lambda b, n, m: (0, 0, 0)),
                pl.BlockSpec((images, seg, enc), lambda b, n, m: (lax.div(image_at(plan, n, m), images), 0, 0)),
            ]
            + unread(deps),
            out_specs=slabs,
            scratch_shapes=[pltpu.VMEM((images * seg, width), jnp.bfloat16)],
        ),
        out_shape=slab_shapes(split, ranks, (per, seg, HD)),
        cost_estimate=cost(
            4 * images * seg * width * enc, 2 * width * enc + 10 * images * seg * width, 0
        ),
        compiler_params=pltpu.CompilerParams(vmem_limit_bytes=VMEM_LIMIT),
        name="align_head",
    )(*where, *back, whole, target, *deps)


def shards(queries, key_states, value_states, projector, teacher, enc_gain, enc_bias, valid_len):
    ranks = lax.axis_size("seq")
    count, seg, width = queries.shape
    heads = width // HD
    images = 1
    while images * heads % ranks:
        images *= 2
    chunks = count // images
    per = images * heads // ranks
    rank = lax.axis_index("seq").astype(jnp.int32)

    first_image = (lax.axis_index("grp") * lax.axis_size("dp") + lax.axis_index("dp")) * count
    where = (valid_len, jnp.stack([rank, rank * seg, first_image.astype(jnp.int32)]))
    plans = [(c, chunks, images) for c in range(chunks)]
    split = [chunks > 1 and c == chunks - 1 for c in range(chunks)]

    arrays = (queries, key_states, value_states)
    packed = []
    for c in range(chunks):
        deps = [slabs[0] for slabs in packed]
        packed.append(pack(arrays, plans[c], ranks, per, split[c], where, deps))
    normed = layer_norm(teacher, enc_gain, enc_bias, packed[0][0])
    target = from_partner(normed, "grp", 0)
    whole = gather_rows(projector, packed[-1][:1])

    def ahead(near, made, c, also=[]):
        if not split[-1]:
            return []
        return made[c - 1][:1] if split[c] else near[-1][:3] + also

    qkv = [exchange(slabs) for slabs in packed]
    attended, kept = [], []
    for c in range(chunks):
        slabs, state = forward(qkv[c], plans[c], ranks, where, ahead(qkv, attended, c, [target]))
        kept.append(state)
        attended.append(slabs)
    back = [exchange(slabs) for slabs in attended]
    grad_rows = []
    for c in range(chunks):
        deps = ahead(back, grad_rows, c)
        grad_rows.append(align_head(back[c], whole, target, plans[c], ranks, where, deps))
    g_in = [exchange(slabs) for slabs in grad_rows]
    grads = []
    for c in range(chunks):
        deps = ahead(g_in, grads, c)
        grads.append(backward(qkv[c], g_in[c], kept[c], plans[c], ranks, where, deps))
    grads = [exchange(slabs) for slabs in grads]
    outs = ()
    for c in range(chunks):
        if not split[c]:
            outs = unpack(grads[c][0], plans[c], count, where, outs, ahead(grads, None, c))
            continue
        for s, slab in enumerate(grads[c]):
            outs = place(slab, s, plans[c], count, ranks, where, outs)
    return tuple(outs)


def solution(mesh):
    return jax.shard_map(
        shards,
        mesh=mesh,
        in_specs=(
            P(("grp", "dp"), "seq", None),
            P(("grp", "dp"), "seq", None),
            P(("grp", "dp"), "seq", None),
            P("seq", None),
            P(("grp", "dp"), "seq", None),
            P(),
            P(),
            P(),
        ),
        out_specs=(
            P(("grp", "dp"), "seq", None),
            P(("grp", "dp"), "seq", None),
            P(("grp", "dp"), "seq", None),
        ),
        check_vma=False,
    )
```
